32 devices in a mesh: fsdp: 4 (over y, core), ctx: 8 (over z, x).
Axes of the slice: x: 2, y: 2, z: 4, core: 2. Of those that a mesh axis runs over, the one named last changes fastest.
Arguments:
- featurized: bfloat16 [1024, 3, 4096], P('ctx', None, 'fsdp'), may hold values from -6 to 6
- short_taps: float32 [3, 3, 4096], P(None, None, 'fsdp'), may hold values from -3 to 3
- residues: float32 [4096, 16], P('fsdp'), may hold values from -1.5 to 1.5
- decay_rates: float32 [4096, 16], P('fsdp'), may hold values from 0.00048828125 to 0.05
- w_out: bfloat16 [4096, 8192], P('fsdp', 'ctx'), may hold values from -0.09375 to 0.09375
- grad_out: bfloat16 [1024, 8192], P('ctx'), may hold values from -6 to 6
Outputs:
- block_output: bfloat16 [1024, 8192], P('ctx', 'fsdp')
- grad_features: bfloat16 [1024, 3, 4096], P('ctx', None, 'fsdp')
The draws below stay inside these ranges and needn't reach their ends.
All inputs are finite; a program needn't handle non-finite values.
Results may differ from the reference program's by a relative error of at most 0.02.
Values may be sent and summed in bfloat16 or wider, within the bound.
No kernel may reach another device: no remote copies, remote signals or barrier semaphores. Data moves between devices by JAX's collectives and lax.ppermute only.
A program may use at most 128 MiB of HBM per device.

```python
import math
import jax
import jax.numpy as jnp
from jax import lax

D = 8192
H = 4096
STATE = 16
SEQ = 1024
N_FSDP = 4


def level_of(own_key, extent, pieces, low, largest):
    loudness = 1.0
    for dim, shards_of in pieces:
        steps = jax.random.uniform(jax.random.fold_in(jax.random.fold_in(own_key, 6), dim), (shards_of,), jnp.float32, low / len(pieces), largest / len(pieces))
        loudness = loudness * jnp.repeat(jnp.exp(steps), extent[dim] // shards_of).reshape((-1,) + (1,) * (len(extent) - 1 - dim))
    return loudness


def scatter_about(stream_key, extent, width, bound, pieces=(), held_as=jnp.bfloat16):
    array = width * jax.random.normal(stream_key, extent, jnp.float32)
    if pieces:
        array = array * level_of(stream_key, extent, pieces, -0.22, 0.18)
    return jnp.clip(array, -bound, bound).astype(held_as)


def setup_inputs(seed: int = 0) -> dict:
    seeds = jax.random.split(jax.random.key(seed), 7)
    return {
        "featurized": scatter_about(seeds[0], (SEQ, 3, H), 1.0, 6.0, ((0, 8), (2, 4))),
        "short_taps": scatter_about(seeds[1], (3, 3, H), 0.6, 3.0, ((2, 4),), jnp.float32),
        "residues": scatter_about(seeds[2], (H, STATE), 0.25, 1.5, ((0, 4),), jnp.float32),
        "decay_rates": jnp.clip(jnp.exp(math.log(0.05) - 4.6288867 * jax.random.uniform(seeds[3], (H, STATE), jnp.float32) ** level_of(seeds[3], (H, STATE), ((0, 4),), -0.2, 0.2)), 0.00048828125, 0.05),
        "w_out": scatter_about(seeds[4], (H, D), H ** -0.5, 0.09375, ((0, 4), (1, 8))),
        "grad_out": scatter_about(seeds[5], (SEQ, D), 1.0, 6.0, ((0, 8),)),
    }


def impulse_taps(residues, decay_rates):
    positions = jnp.arange(SEQ).astype(jnp.float32)
    total_now = jnp.zeros((SEQ, H), jnp.float32)
    for mode_index in range(STATE):
        rates_now = decay_rates[:, mode_index]
        weight = residues[:, mode_index] * jnp.sqrt(rates_now)
        total_now = total_now + weight[None, :] * jnp.exp(-positions[:, None] * rates_now[None, :])
    return total_now

def causal_taps(signal, short_taps):
    padded = jnp.pad(signal, ((2, 0), (0, 0), (0, 0)))
    return short_taps[0] * padded[2:] + short_taps[1] * padded[1:-1] + short_taps[2] * padded[:-2]

def causal_adjoint(signal, short_taps):
    padded = jnp.pad(signal, ((0, 2), (0, 0), (0, 0)))
    return short_taps[0] * padded[:-2] + short_taps[1] * padded[1:-1] + short_taps[2] * padded[2:]

def spectrum(signal):
    return jnp.fft.rfft(signal, n=2 * SEQ, axis=0)

def from_spectrum(values):
    return jnp.fft.irfft(values, n=2 * SEQ, axis=0)[:SEQ]

def reference(featurized, short_taps, residues, decay_rates, w_out, grad_out):
    raw_values = featurized.astype(jnp.float32)
    mixed_in = causal_taps(raw_values, short_taps)
    query_part = mixed_in[:, 0]
    key_part = mixed_in[:, 1]
    value_part = mixed_in[:, 2]
    carried = key_part * value_part
    filter_spec = spectrum(impulse_taps(residues, decay_rates))
    convolved = from_spectrum(filter_spec * spectrum(carried))
    gated_out = (query_part * convolved).astype(jnp.bfloat16)
    group_width = H // N_FSDP
    total_now = jnp.zeros((SEQ, D), jnp.float32)
    for group_index in range(N_FSDP):
        group_term = jnp.dot(gated_out[:, group_index * group_width:(group_index + 1) * group_width], w_out[group_index * group_width:(group_index + 1) * group_width], preferred_element_type=jnp.float32)
        total_now = total_now + lax.optimization_barrier(group_term.astype(jnp.bfloat16)).astype(jnp.float32)
    block_output = total_now.astype(jnp.bfloat16)
    grad_gated = jnp.dot(grad_out, w_out.T, preferred_element_type=jnp.float32)
    grad_query = grad_gated * convolved
    grad_conv = grad_gated * query_part
    grad_carried = from_spectrum(jnp.conj(filter_spec) * spectrum(grad_conv))
    grad_mixed = jnp.stack([grad_query, grad_carried * value_part, grad_carried * key_part], axis=1)
    grad_features = causal_adjoint(grad_mixed, short_taps).astype(jnp.bfloat16)
    return (block_output, grad_features)
```

```python
import functools

import jax
import jax.numpy as jnp
from jax import lax
from jax.experimental import pallas as pl
from jax.experimental.pallas import tpu as pltpu
from jax.sharding import PartitionSpec as P

LANES = 128
F32 = jnp.float32
BF16 = jnp.bfloat16
VMEM = pl.BlockSpec(memory_space=pltpu.VMEM)
SMEM = pl.BlockSpec(memory_space=pltpu.SMEM)


def swapped(block, axis, mask):
    count = lax.axis_size(axis)
    return lax.ppermute(block, axis, [(i, i ^ mask) for i in range(count)])


def shifted(block, axis, distance):
    devices = range(lax.axis_size(axis))
    route = [(i - distance, i) for i in devices if i - distance in devices]
    return lax.ppermute(block, axis, route)


def tree_sum(terms):
    terms = list(terms)
    while len(terms) > 1:
        paired = [terms[i] + terms[i + 1] for i in range(0, len(terms) - 1, 2)]
        terms = paired + terms[len(terms) - len(terms) % 2 :]
    return terms[0]


def kernel_call(body, out_shape, in_specs, scratch_shapes=(), flops=0, moved=0):
    return pl.pallas_call(
        body,
        out_shape=out_shape,
        in_specs=in_specs,
        out_specs=jax.tree.map(lambda _: VMEM, out_shape),
        scratch_shapes=scratch_shapes,
        compiler_params=pltpu.CompilerParams(vmem_limit_bytes=48 * 1024 * 1024),
        cost_estimate=pl.CostEstimate(flops=flops, bytes_accessed=moved, transcendentals=0),
    )


def chunk_state_kernel(tokens, x_ref, taps_ref, rates_ref, mixed_ref, state_ref):
    modes = rates_ref.shape[0]
    decays = [jnp.exp(-rates_ref[n]) for n in range(modes)]

    def mix(t):
        parts = []
        for j in range(3):
            part = (
                taps_ref[0, j] * x_ref[t + 2, j]
                + taps_ref[1, j] * x_ref[t + 1, j]
                + taps_ref[2, j] * x_ref[t, j]
            )
            mixed_ref[t, j] = part
            parts.append(part)
        return parts[1] * parts[2]

    def step(t, states):
        carried = mix(t)
        return tuple(decays[n] * states[n] + carried for n in range(modes))

    empty = jnp.zeros(state_ref.shape[1:], F32)
    states = lax.fori_loop(0, tokens, step, (empty,) * modes, unroll=4)
    for n in range(modes):
        state_ref[n] = states[n]
    mix(tokens)
    mix(tokens + 1)


def incoming(tokens, rates, arrived, distance_ref, n):
    total = None
    for k, block in enumerate(arrived):
        reach = jnp.exp(-rates * (tokens * distance_ref[0, k])) * distance_ref[1, k]
        term = reach * block[n].astype(F32)
        total = term if total is None else total + term
    return total


def convolve_kernel(tokens, peers, distance_ref, rates_ref, residues_ref, mixed_ref, *refs):
    arrived, (gated_ref, convolved_ref, rows_ref) = refs[:peers], refs[peers:]
    modes, tall = rates_ref.shape[0], rates_ref.shape[1]
    decays = [jnp.exp(-rates_ref[n]) for n in range(modes)]
    weights = [residues_ref[n] * jnp.sqrt(rates_ref[n]) for n in range(modes)]
    states = tuple(
        incoming(tokens, rates_ref[n], arrived, distance_ref, n) for n in range(modes)
    )

    def advance(t, states):
        carried = mixed_ref[t, 1] * mixed_ref[t, 2]
        states = tuple(decays[n] * states[n] + carried for n in range(modes))
        convolved = tree_sum([weights[n] * states[n] for n in range(modes)])
        convolved_ref[t] = convolved
        return states, convolved

    def step(t, states):
        states, convolved = advance(t, states)
        rows_ref[pl.ds(pl.multiple_of(t * tall, tall), tall), :] = mixed_ref[t, 0] * convolved
        return states

    states = lax.fori_loop(0, tokens, step, states, unroll=4)
    states, _ = advance(tokens, states)
    advance(tokens + 1, states)
    for start in range(0, tokens, 16):
        for s in range(tall):
            rows = rows_ref[pl.ds(start * tall + s, 16, stride=tall), :]
            gated_ref[start : start + 16, s * LANES : (s + 1) * LANES] = rows.astype(BF16)


def back_state_kernel(tokens, peers, half_ref, rates_ref, mixed_ref, *refs):
    terms, (grads_ref, state_ref, head_ref) = refs[: peers + 1], refs[peers + 1 :]
    modes, tall = rates_ref.shape[0], rates_ref.shape[1]
    decays = [jnp.exp(-rates_ref[n]) for n in range(modes)]
    offset = half_ref[0] * (tokens // 2)
    for start in range(0, tokens, 16):
        own = pl.multiple_of((start + offset) % tokens, 16)
        for s in range(tall):
            lanes = slice(s * LANES, (s + 1) * LANES)
            total = tree_sum([term[pl.ds(own, 16), lanes].astype(F32) for term in terms])
            grads_ref[pl.ds(start * tall + s, 16, stride=tall), :] = total

    def step(i, states):
        t = tokens - 1 - i
        here = grads_ref[pl.ds(pl.multiple_of(t * tall, tall), tall), :] * mixed_ref[t, 0]
        return tuple(decays[n] * states[n] + here for n in range(modes))

    empty = jnp.zeros(state_ref.shape[1:], F32)
    states = lax.fori_loop(0, tokens, step, (empty,) * modes, unroll=4)
    for n in range(modes):
        state_ref[n] = states[n].astype(state_ref.dtype)
    head_ref[0] = grads_ref[0:tall, :]
    head_ref[1] = grads_ref[tall : 2 * tall, :]


def adjoint_kernel(
    tokens, peers, distance_ref, rates_ref, residues_ref, taps_ref, mixed_ref, convolved_ref,
    grads_ref, after_ref, *refs
):
    arrived, (out_ref,) = refs[:peers], refs[peers:]
    modes, tall = rates_ref.shape[0], rates_ref.shape[1]
    decays = [jnp.exp(-rates_ref[n]) for n in range(modes)]
    weights = [residues_ref[n] * jnp.sqrt(rates_ref[n]) for n in range(modes)]

    def spread(t, grad, states):
        grad_carried = tree_sum([weights[n] * states[n] for n in range(modes)])
        return (
            grad * convolved_ref[t],
            grad_carried * mixed_ref[t, 2],
            grad_carried * mixed_ref[t, 1],
        )

    states = tuple(
        incoming(tokens, rates_ref[n], arrived, distance_ref, n) for n in range(modes)
    )
    first = spread(tokens, after_ref[0], states)
    after_that = tuple(
        (states[n] - after_ref[0] * mixed_ref[tokens, 0]) * jnp.exp(rates_ref[n])
        for n in range(modes)
    )
    second = spread(tokens + 1, after_ref[1], after_that)

    def step(i, carry):
        states, first, second = carry
        t = tokens - 1 - i
        grad = grads_ref[pl.ds(pl.multiple_of(t * tall, tall), tall), :]
        here = grad * mixed_ref[t, 0]
        states = tuple(decays[n] * states[n] + here for n in range(modes))
        mine = spread(t, grad, states)
        for j in range(3):
            out_ref[t, j] = (
                taps_ref[0, j] * mine[j] + taps_ref[1, j] * first[j] + taps_ref[2, j] * second[j]
            )
        return states, mine, first

    lax.fori_loop(0, tokens, step, (states, first, second), unroll=4)


def per_device(featurized, short_taps, residues, decay_rates, w_out, grad_out):
    tokens, _, wide = featurized.shape
    tall = wide // LANES
    modes = residues.shape[1]
    n_ctx, n_fsdp = lax.axis_size("ctx"), lax.axis_size("fsdp")
    me, group = lax.axis_index("ctx"), lax.axis_index("fsdp")
    pair, side = me // 2, me % 2
    core, line = group % 2, group // 2
    n_pair, n_line = n_ctx // 2, n_fsdp // 2
    width = w_out.shape[1]
    half = tokens // 2
    masks = range(1, n_ctx)

    before = shifted(featurized[tokens - 2 :], "ctx", 1)
    after = shifted(featurized[:2], "ctx", -1)

    own_rows = lax.dynamic_slice_in_dim(grad_out, core * half, half, 0)

    def columns(source, owner_pair):
        mine = lax.dynamic_slice_in_dim(source, (2 * owner_pair + side) * width, width, 1)
        other = lax.dynamic_slice_in_dim(source, (2 * owner_pair + 1 - side) * width, width, 1)
        return mine, other

    near = [None] * n_pair
    for k in range(1, n_pair):
        near[k] = swapped(jnp.concatenate(columns(own_rows, pair ^ k), axis=1), "ctx", 2 * k)
    far = [None] + [swapped(near[k], "fsdp", 1) for k in range(1, n_pair)]
    w_other = swapped(w_out, "ctx", 1)

    extended = jnp.concatenate([before, featurized, after], axis=0).astype(F32)
    extended = extended.reshape(tokens + 4, 3, tall, LANES)
    taps = short_taps.reshape(3, 3, tall, LANES)
    rates = decay_rates.T.reshape(modes, tall, LANES)
    weights = residues.T.reshape(modes, tall, LANES)
    state_shape = jax.ShapeDtypeStruct((modes, tall, LANES), F32)
    mixed, state = kernel_call(
        functools.partial(chunk_state_kernel, tokens),
        (jax.ShapeDtypeStruct((tokens + 2, 3, tall, LANES), F32), state_shape),
        [VMEM] * 3,
        flops=50 * tokens * wide,
        moved=8 * tokens * 3 * wide,
    )(extended, taps, rates)
    arrived = [swapped(state, "ctx", k) for k in masks]
    partners = me ^ jnp.arange(1, n_ctx)
    ahead = me - partners
    distance = jnp.stack([jnp.maximum(ahead - 1, 0), ahead > 0]).astype(F32)
    back_distance = jnp.stack([jnp.maximum(-ahead - 1, 0), ahead < 0]).astype(F32)
    gated, convolved = kernel_call(
        functools.partial(convolve_kernel, tokens, len(arrived)),
        (
            jax.ShapeDtypeStruct((tokens, wide), BF16),
            jax.ShapeDtypeStruct((tokens + 2, tall, LANES), F32),
        ),
        [SMEM] + [VMEM] * (3 + len(arrived)),
        [pltpu.VMEM((tokens * tall, LANES), F32)],
        flops=64 * tokens * wide,
        moved=8 * tokens * 3 * wide,
    )(distance, rates, weights, mixed, *arrived)

    blocks = jnp.stack([gated] + [swapped(gated, "ctx", 2 * k) for k in range(1, n_pair)])
    kept = lax.dynamic_slice_in_dim(blocks, core * n_line, n_line, 0)
    given = lax.dynamic_slice_in_dim(blocks, (1 - core) * n_line, n_line, 0)
    route = []
    for f in range(n_fsdp):
        for p in range(n_pair):
            for x in range(2):
                target = p ^ ((f % 2) * n_line + f // 2)
                route.append((f * n_ctx + 2 * p + x, p * n_ctx + 2 * target + x))

    def project(columns_here):
        product = functools.partial(
            lax.dot_general,
            dimension_numbers=(((2,), (0,)), ((), ())),
            preferred_element_type=F32,
        )
        sent = swapped(product(given, columns_here).astype(BF16), "fsdp", 1)
        summed = product(kept, columns_here) + sent.astype(F32)
        total = lax.dynamic_index_in_dim(summed, line, 0, False)
        for m in range(1, n_line):
            block = lax.dynamic_index_in_dim(summed, line ^ m, 0, False).astype(BF16)
            total = total + swapped(block, "fsdp", 2 * m).astype(F32)
        return lax.ppermute(total.astype(BF16), ("fsdp", "ctx"), route)

    out_mine, out_other = project(w_out), project(w_other)
    block_output = jnp.where(
        side == 0,
        jnp.concatenate([out_mine, out_other], axis=1),
        jnp.concatenate([out_other, out_mine], axis=1),
    )

    def pull(rows):
        contract = (((1,), (1,)), ((), ()))
        return lax.dot_general(
            rows[:, :width], w_out, contract, preferred_element_type=F32
        ) + lax.dot_general(rows[:, width:], w_other, contract, preferred_element_type=F32)

    terms = []
    for k in range(1, n_pair):
        term = jnp.concatenate([pull(near[k]), pull(far[k])], axis=0).astype(BF16)
        terms.append(swapped(term, "ctx", 2 * k))
    mine, other = columns(grad_out, pair)
    rest = lax.dynamic_slice_in_dim(grad_out, (1 - core) * half, half, 0)
    here = jnp.concatenate([own_rows, rest], axis=0)
    own = pull(jnp.concatenate(columns(here, pair), axis=1))
    grads, back_state, head = kernel_call(
        functools.partial(back_state_kernel, tokens, len(terms)),
        (
            jax.ShapeDtypeStruct((tokens * tall, LANES), F32),
            state_shape,
            jax.ShapeDtypeStruct((2, tall, LANES), F32),
        ),
        [SMEM] + [VMEM] * (3 + len(terms)),
        flops=40 * tokens * wide,
        moved=8 * tokens * 3 * wide,
    )(core[None].astype(jnp.int32), rates, mixed, own, *terms)
    back_arrived = [swapped(back_state, "ctx", k) for k in masks]
    following = shifted(head, "ctx", -1)
    out = kernel_call(
        functools.partial(adjoint_kernel, tokens, len(back_arrived)),
        (jax.ShapeDtypeStruct((tokens, 3, tall, LANES), F32),),
        [SMEM] + [VMEM] * (7 + len(back_arrived)),
        flops=80 * tokens * wide,
        moved=8 * tokens * 3 * wide,
    )(
        back_distance, rates, weights, taps, mixed, convolved, grads, following, *back_arrived
    )[0]
    grad_features = out.reshape(tokens, 3, wide).astype(BF16)
    return (block_output, grad_features)


def solution(mesh):
    placed = (
        P("ctx", None, "fsdp"),
        P(None, None, "fsdp"),
        P("fsdp", None),
        P("fsdp", None),
        P("fsdp", "ctx"),
        P("ctx", None),
    )
    return jax.shard_map(
        per_device,
        mesh=mesh,
        in_specs=placed,
        out_specs=(P("ctx", "fsdp"), P("ctx", None, "fsdp")),
        check_vma=False,
    )
```

```python
import functools

import jax
import jax.numpy as jnp
from jax import lax
from jax.experimental import pallas as pl
from jax.experimental.pallas import tpu as pltpu
from jax.sharding import PartitionSpec as P

LANES = 128
F32 = jnp.float32
BF16 = jnp.bfloat16
VMEM = pl.BlockSpec(memory_space=pltpu.VMEM)
SMEM = pl.BlockSpec(memory_space=pltpu.SMEM)
HBM = pl.BlockSpec(memory_space=pltpu.HBM)
ANYWHERE = pl.BlockSpec(memory_space=pl.ANY)


def swapped(block, axis, mask):
    count = lax.axis_size(axis)
    return lax.ppermute(block, axis, [(i, i ^ mask) for i in range(count)])


def shifted(block, axis, distance):
    devices = range(lax.axis_size(axis))
    route = [(i - distance, i) for i in devices if i - distance in devices]
    return lax.ppermute(block, axis, route)


def tree_sum(terms):
    terms = list(terms)
    while len(terms) > 1:
        paired = [terms[i] + terms[i + 1] for i in range(0, len(terms) - 1, 2)]
        terms = paired + terms[len(terms) - len(terms) % 2 :]
    return terms[0]


def kernel_call(body, out_shape, in_specs, scratch_shapes=(), flops=0, moved=0):
    return pl.pallas_call(
        body,
        out_shape=out_shape,
        in_specs=in_specs,
        out_specs=jax.tree.map(lambda _: VMEM, out_shape),
        scratch_shapes=scratch_shapes,
        compiler_params=pltpu.CompilerParams(vmem_limit_bytes=48 * 1024 * 1024),
        cost_estimate=pl.CostEstimate(flops=flops, bytes_accessed=moved, transcendentals=0),
    )


def chunk_state_kernel(tokens, x_ref, before_ref, taps_ref, rates_ref, mixed_ref, state_ref):
    modes = rates_ref.shape[0]
    decays = [jnp.exp(-rates_ref[n]) for n in range(modes)]

    def mix(t, rows):
        parts = []
        for j in range(3):
            part = tree_sum([taps_ref[i, j] * rows[i][j] for i in range(3)])
            mixed_ref[t, j] = part
            parts.append(part)
        return parts[1] * parts[2]

    def absorb(states, carried):
        return tuple(decays[n] * states[n] + carried for n in range(modes))

    def step(t, states):
        return absorb(states, mix(t, [x_ref.at[t - i] for i in range(3)]))

    states = (jnp.zeros(state_ref.shape[1:], F32),) * modes
    states = absorb(states, mix(0, [x_ref.at[0], before_ref.at[1], before_ref.at[0]]))
    states = absorb(states, mix(1, [x_ref.at[1], x_ref.at[0], before_ref.at[1]]))
    states = lax.fori_loop(2, tokens, step, states, unroll=3)
    for n in range(modes):
        state_ref[n] = states[n]


def incoming(rates, arrived, reach_ref, n):
    terms = []
    for k, block in enumerate(arrived):
        terms.append(jnp.exp(-rates * reach_ref[0, k]) * reach_ref[1, k] * block[n])
    return tree_sum(terms)


def convolve_kernel(tokens, peers, reach_ref, rates_ref, residues_ref, mixed_ref, *refs):
    arrived, (gated_ref, convolved_ref, rows_ref) = refs[:peers], refs[peers:]
    modes, tall = rates_ref.shape[0], rates_ref.shape[1]
    decays = [jnp.exp(-rates_ref[n]) for n in range(modes)]
    weights = [residues_ref[n] * jnp.sqrt(rates_ref[n]) for n in range(modes)]
    states = tuple(incoming(rates_ref[n], arrived, reach_ref, n) for n in range(modes))

    def step(t, states):
        carried = mixed_ref[t, 1] * mixed_ref[t, 2]
        states = tuple(decays[n] * states[n] + carried for n in range(modes))
        convolved = tree_sum([weights[n] * states[n] for n in range(modes)])
        convolved_ref[t] = convolved
        rows_ref[pl.ds(pl.multiple_of(t * tall, tall), tall), :] = mixed_ref[t, 0] * convolved
        return states

    lax.fori_loop(0, tokens, step, states, unroll=4)
    for start in range(0, tokens, 16):
        for s in range(tall):
            rows = rows_ref[pl.ds(start * tall + s, 16, stride=tall), :]
            gated_ref[start : start + 16, s * LANES : (s + 1) * LANES] = rows.astype(BF16)


def back_state_kernel(tokens, peers, rates_ref, mixed_ref, convolved_ref, own_ref, *refs):
    sources, (grads_ref, state_ref, head_ref) = refs[:peers], refs[peers : peers + 3]
    terms, sems = refs[peers + 3 : -1], refs[-1]
    copies = []
    for k in range(peers):
        copies.append(pltpu.make_async_copy(sources[k], terms[k], sems.at[k]))
        copies[k].start()
    modes, tall = rates_ref.shape[0], rates_ref.shape[1]
    decays = [jnp.exp(-rates_ref[n]) for n in range(modes)]
    for copy in copies:
        copy.wait()
    for start in range(0, tokens, 16):
        for s in range(tall):
            lanes = slice(s * LANES, (s + 1) * LANES)
            parts = [term[start : start + 16, lanes].astype(F32) for term in terms]
            total = tree_sum([own_ref[start : start + 16, lanes]] + parts)
            grads_ref[pl.ds(start * tall + s, 16, stride=tall), :] = total

    def step(i, states):
        t = tokens - 1 - i
        here = grads_ref[pl.ds(pl.multiple_of(t * tall, tall), tall), :] * mixed_ref[t, 0]
        return tuple(decays[n] * states[n] + here for n in range(modes))

    empty = jnp.zeros(state_ref.shape[1:], F32)
    states = lax.fori_loop(0, tokens, step, (empty,) * modes, unroll=4)
    for n in range(modes):
        state_ref[n] = states[n]
    for t in range(2):
        head_ref[t, 0] = grads_ref[t * tall : (t + 1) * tall, :]
        head_ref[t, 1] = convolved_ref[t]
        for j in range(3):
            head_ref[t, 2 + j] = mixed_ref[t, j]


def adjoint_kernel(
    tokens, peers, reach_ref, rates_ref, residues_ref, taps_ref, mixed_ref, convolved_ref,
    grads_ref, after_ref, *refs
):
    arrived, (out_ref,) = refs[:peers], refs[peers:]
    modes, tall = rates_ref.shape[0], rates_ref.shape[1]
    decays = [jnp.exp(-rates_ref[n]) for n in range(modes)]
    weights = [residues_ref[n] * jnp.sqrt(rates_ref[n]) for n in range(modes)]

    def spread(grad, convolved, mixed, states):
        grad_carried = tree_sum([weights[n] * states[n] for n in range(modes)])
        return (grad * convolved, grad_carried * mixed[2], grad_carried * mixed[1])

    def spread_after(t, states):
        mixed = [after_ref[t, 2 + j] for j in range(3)]
        return spread(after_ref[t, 0], after_ref[t, 1], mixed, states)

    states = tuple(incoming(rates_ref[n], arrived, reach_ref, n) for n in range(modes))
    first = spread_after(0, states)
    beyond = after_ref[0, 0] * after_ref[0, 2]
    second = spread_after(
        1, tuple((states[n] - beyond) * jnp.exp(rates_ref[n]) for n in range(modes))
    )

    def step(i, carry):
        states, first, second = carry
        t = tokens - 1 - i
        grad = grads_ref[pl.ds(pl.multiple_of(t * tall, tall), tall), :]
        here = grad * mixed_ref[t, 0]
        states = tuple(decays[n] * states[n] + here for n in range(modes))
        mine = spread(grad, convolved_ref[t], mixed_ref.at[t], states)
        for j in range(3):
            out_ref[t, j] = (
                taps_ref[0, j] * mine[j] + taps_ref[1, j] * first[j] + taps_ref[2, j] * second[j]
            )
        return states, mine, first

    lax.fori_loop(0, tokens, step, (states, first, second), unroll=4)


def fetched(pairs, sems):
    copies = []
    for source, target in pairs:
        copies.append(pltpu.make_async_copy(source, target, sems.at[len(copies)]))
        copies[-1].start()
    return copies


def stacked(pieces, target):
    pairs, at = [], 0
    for piece in pieces:
        pairs.append((piece, target.at[pl.ds(at, piece.shape[0]), :]))
        at += piece.shape[0]
    return pairs


def product_kernel(n_pair, n_line, pieces, place_ref, own_src, mine_src, *refs):
    others, arrived = refs[:pieces], refs[pieces : pieces + 4]
    blocks, outs = refs[pieces + 4 : pieces + 4 + n_pair], refs[pieces + 4 + n_pair : -5]
    own_ref, other_ref, rows_ref, gated_ref, sems = refs[-5:]
    core, turn, side, pair = [place_ref[i] for i in range(4)]
    tokens, (wide, width) = mine_src.shape[0], own_src.shape
    part = tokens // 4
    columns = pl.ds(pl.multiple_of(pair * 2 * width, 2 * width), 2 * width)
    pairs = [(own_src, own_ref), (mine_src.at[:, columns], rows_ref.at[pl.ds(0, tokens), :])]
    turns = (2 * turn, 2 * (1 - turn), 2 * turn, 2 * (1 - turn))
    cores = (core, core, 1 - core, 1 - core)
    for k in range(1, n_pair):
        for block, up, across in zip(arrived, turns, cores):
            at = pl.multiple_of(k * tokens + (up + across) * part, part)
            source = block.at[pl.ds((k - 1) * part, part), :]
            pairs.append((source, rows_ref.at[pl.ds(at, part), :]))
    early, pairs = len(pairs), pairs + stacked(others, other_ref)
    middle, pairs = len(pairs), pairs + stacked(blocks, gated_ref)
    copies = fetched(pairs, sems)
    for copy in copies[:early]:
        copy.wait()
    contract = (((1,), (1,)), ((), ()))
    step = min(256, wide)
    halves = ((own_ref, side), (other_ref, 1 - side))
    for n in range(0, wide, step):
        parts = []
        for w_ref, at in halves:
            if n == 0 and w_ref is other_ref:
                for copy in copies[early:middle]:
                    copy.wait()
            rows = rows_ref[:, pl.ds(pl.multiple_of(at * width, width), width)]
            w = w_ref[n : n + step, :]
            parts.append(lax.dot_general(rows, w, contract, preferred_element_type=F32))
        total = parts[0] + parts[1]
        for k, out_ref in enumerate(outs[2:]):
            here = total[k * tokens : (k + 1) * tokens]
            out_ref[:, n : n + step] = here.astype(out_ref.dtype)
    for copy in copies[middle:]:
        copy.wait()
    step = min(256, width)
    tall = n_line * tokens
    for out_ref, half in ((outs[0], 1 - core), (outs[1], core)):
        rows = gated_ref[pl.ds(pl.multiple_of(half * tall, tall), tall), :]
        for w_ref, at in halves:
            for n in range(0, width, step):
                product = jnp.dot(rows, w_ref[:, n : n + step], preferred_element_type=F32)
                columns = pl.ds(pl.multiple_of(at * width + n, step), step)
                out_ref[:, columns] = product.astype(BF16)


def per_device(featurized, short_taps, residues, decay_rates, w_out, grad_out):
    tokens, _, wide = featurized.shape
    tall = wide // LANES
    modes = residues.shape[1]
    n_ctx, n_fsdp = lax.axis_size("ctx"), lax.axis_size("fsdp")
    me, group = lax.axis_index("ctx"), lax.axis_index("fsdp")
    pair, side = me // 2, me % 2
    core, line = group % 2, group // 2
    n_pair, n_line = n_ctx // 2, n_fsdp // 2
    width = w_out.shape[1]
    turn, part = line % 2, tokens // 4
    place = jnp.stack([core, turn, side, pair]).astype(jnp.int32)

    before = shifted(featurized[tokens - 2 :], "ctx", 1)

    near_cut = []
    for k in range(1, n_pair):
        at = ((2 * turn + core) * part, (pair ^ k) * 2 * width)
        block = lax.dynamic_slice(grad_out, at, (part, 2 * width))
        near_cut.append(block)

    def tiled(rows):
        return rows.astype(F32).reshape(-1, 3, tall, LANES)

    taps = tiled(short_taps)
    rates = decay_rates.T.reshape(modes, tall, LANES)
    weights = residues.T.reshape(modes, tall, LANES)
    state_shape = jax.ShapeDtypeStruct((modes, tall, LANES), F32)
    levels = range(n_ctx.bit_length() - 1)
    uppers = [(me >> b) % 2 for b in levels]
    belows = [me % (1 << b) for b in levels]

    def exchanged(total, later, others=()):
        arrived = []
        for b in levels:
            partner = swapped(total, "ctx", 1 << b)
            if others and b == 0:
                partner, others = lax.optimization_barrier((partner, others))
            arrived.append(partner)
            if b + 1 < len(levels):
                decay = jnp.exp(-rates * (tokens << b))
                fades = (uppers[b] == 0) == later
                total = jnp.where(fades, total * decay + partner, partner * decay + total)
        return (arrived, others) if others else arrived

    reach = jnp.stack([
        jnp.stack([below * tokens for below in belows]),
        jnp.stack([upper == 1 for upper in uppers]),
    ]).astype(F32)
    back_reach = jnp.stack([
        jnp.stack([((1 << b) - 1 - belows[b]) * tokens for b in levels]),
        jnp.stack([upper == 0 for upper in uppers]),
    ]).astype(F32)

    mixed, state = kernel_call(
        functools.partial(chunk_state_kernel, tokens),
        (jax.ShapeDtypeStruct((tokens, 3, tall, LANES), F32), state_shape),
        [VMEM] * 4,
        flops=50 * tokens * wide,
        moved=8 * tokens * 3 * wide,
    )(tiled(featurized), tiled(before), taps, rates)
    w_held, state = lax.optimization_barrier((w_out, state))
    arrived = exchanged(state, True)
    w_held, _ = lax.optimization_barrier((w_out, arrived[0]))
    w_other = [swapped(w_held, "ctx", 1)]
    near_cut, _ = lax.optimization_barrier((near_cut, arrived[2]))
    near = [swapped(block, "ctx", 2 * k) for k, block in enumerate(near_cut, 1)]
    gated, convolved = kernel_call(
        functools.partial(convolve_kernel, tokens, len(arrived)),
        (
            jax.ShapeDtypeStruct((tokens, wide), BF16),
            jax.ShapeDtypeStruct((tokens, tall, LANES), F32),
        ),
        [SMEM] + [VMEM] * (3 + len(arrived)),
        [pltpu.VMEM((tokens * tall, LANES), F32)],
        flops=64 * tokens * wide,
        moved=8 * tokens * 3 * wide,
    )(reach, rates, weights, mixed, *arrived)

    blocks = [gated] + [swapped(gated, "ctx", 2 * k) for k in range(1, n_pair)]
    near, _ = lax.optimization_barrier((near, gated))
    near = jnp.concatenate(near, axis=0)
    across = swapped(near, "fsdp", 2)
    far = [swapped(near, "fsdp", 1), swapped(across, "fsdp", 1)]

    route = []
    for f in range(n_fsdp):
        for p in range(n_pair):
            for x in range(2):
                target = p ^ ((f % 2) * n_line + f // 2)
                route.append((f * n_ctx + 2 * p + x, p * n_ctx + 2 * target + x))

    halved = jax.ShapeDtypeStruct((n_line * tokens, 2 * width), BF16)
    given, kept, *outs = kernel_call(
        functools.partial(product_kernel, n_pair, n_line, len(w_other)),
        (halved, halved, jax.ShapeDtypeStruct((tokens, wide), F32))
        + (jax.ShapeDtypeStruct((tokens, wide), BF16),) * (n_pair - 1),
        [SMEM] + [HBM] * (2 + len(w_other)) + [ANYWHERE] * (4 + n_pair),
        [
            pltpu.VMEM((wide, width), BF16),
            pltpu.VMEM((wide, width), BF16),
            pltpu.VMEM((n_pair * tokens, 2 * width), BF16),
            pltpu.VMEM((n_pair * tokens, wide), BF16),
            pltpu.SemaphoreType.DMA((2 + 4 * (n_pair - 1) + len(w_other) + n_pair,)),
        ],
        flops=8 * n_pair * tokens * wide * width,
        moved=8 * wide * width,
    )(place, w_out, grad_out, *w_other, near, across, *far, *blocks)
    terms = [outs[0]] + [swapped(outs[k], "ctx", 2 * k) for k in range(1, n_pair)]

    sent = swapped(given, "fsdp", 1).reshape(n_line, tokens, 2 * width)
    kept = kept.reshape(n_line, tokens, 2 * width)

    def summed(at):
        pieces = [lax.dynamic_index_in_dim(x, at, 0, False).astype(F32) for x in (kept, sent)]
        return pieces[0] + pieces[1]

    total = summed(line)
    rest = [summed(line ^ m).astype(BF16) for m in range(1, n_line)]
    gathered = []
    for at in (0, width):
        part = total[:, at : at + width]
        for m, block in enumerate(rest, 1):
            part = part + swapped(block[:, at : at + width], "fsdp", 2 * m).astype(F32)
        gathered.append(part.astype(BF16))
    terms, _ = lax.optimization_barrier((terms, gathered))
    placed = [lax.ppermute(part, ("fsdp", "ctx"), route) for part in gathered]

    grads, back_state, head = kernel_call(
        functools.partial(back_state_kernel, tokens, n_pair - 1),
        (
            jax.ShapeDtypeStruct((tokens * tall, LANES), F32),
            state_shape,
            jax.ShapeDtypeStruct((2, 5, tall, LANES), F32),
        ),
        [VMEM] * 4 + [ANYWHERE] * (n_pair - 1),
        [pltpu.VMEM((tokens, wide), BF16)] * (n_pair - 1)
        + [pltpu.SemaphoreType.DMA((n_pair - 1,))],
        flops=40 * tokens * wide,
        moved=8 * tokens * 3 * wide,
    )(rates, mixed, convolved, *terms)
    back_arrived, placed = exchanged(back_state, False, placed)
    block_output = jnp.concatenate(placed, axis=1)
    following = shifted(head, "ctx", -1)
    out = kernel_call(
        functools.partial(adjoint_kernel, tokens, len(back_arrived)),
        (jax.ShapeDtypeStruct((tokens, 3, tall, LANES), F32),),
        [SMEM] + [VMEM] * (7 + len(back_arrived)),
        flops=80 * tokens * wide,
        moved=8 * tokens * 3 * wide,
    )(back_reach, rates, weights, taps, mixed, convolved, grads, following, *back_arrived)[0]
    grad_features = out.reshape(tokens, 3, wide).astype(BF16)
    return (block_output, grad_features)


def solution(mesh):
    placed = (
        P("ctx", None, "fsdp"),
        P(None, None, "fsdp"),
        P("fsdp", None),
        P("fsdp", None),
        P("fsdp", "ctx"),
        P("ctx", None),
    )
    return jax.shard_map(
        per_device,
        mesh=mesh,
        in_specs=placed,
        out_specs=(P("ctx", "fsdp"), P("ctx", None, "fsdp")),
        check_vma=False,
    )
```

```python
import functools

import jax
import jax.numpy as jnp
from jax import lax
from jax.experimental import pallas as pl
from jax.experimental.pallas import tpu as pltpu
from jax.sharding import PartitionSpec as P

LANES = 128
F32 = jnp.float32
BF16 = jnp.bfloat16
VMEM = pl.BlockSpec(memory_space=pltpu.VMEM)
SMEM = pl.BlockSpec(memory_space=pltpu.SMEM)
HBM = pl.BlockSpec(memory_space=pltpu.HBM)
ANYWHERE = pl.BlockSpec(memory_space=pl.ANY)


def swapped(block, axis, mask):
    count = lax.axis_size(axis)
    return lax.ppermute(block, axis, [(i, i ^ mask) for i in range(count)])


def shifted(block, axis, distance):
    devices = range(lax.axis_size(axis))
    route = [(i - distance, i) for i in devices if i - distance in devices]
    return lax.ppermute(block, axis, route)


def tree_sum(terms):
    terms = list(terms)
    while len(terms) > 1:
        paired = [terms[i] + terms[i + 1] for i in range(0, len(terms) - 1, 2)]
        terms = paired + terms[len(terms) - len(terms) % 2 :]
    return terms[0]


def kernel_call(body, out_shape, in_specs, scratch_shapes=(), flops=0, moved=0):
    return pl.pallas_call(
        body,
        out_shape=out_shape,
        in_specs=in_specs,
        out_specs=jax.tree.map(lambda _: VMEM, out_shape),
        scratch_shapes=scratch_shapes,
        compiler_params=pltpu.CompilerParams(vmem_limit_bytes=48 * 1024 * 1024),
        cost_estimate=pl.CostEstimate(flops=flops, bytes_accessed=moved, transcendentals=0),
    )


def chunk_state_kernel(tokens, x_ref, before_ref, taps_ref, rates_ref, mixed_ref, state_ref):
    modes = rates_ref.shape[0]
    decays = [jnp.exp(-rates_ref[n]) for n in range(modes)]

    def mix(t, rows):
        parts = []
        for j in range(3):
            part = tree_sum([taps_ref[i, j] * rows[i][j] for i in range(3)])
            mixed_ref[t, j] = part
            parts.append(part)
        return parts[1] * parts[2]

    def absorb(states, carried):
        return tuple(decays[n] * states[n] + carried for n in range(modes))

    def step(t, states):
        return absorb(states, mix(t, [x_ref.at[t - i] for i in range(3)]))

    states = (jnp.zeros(state_ref.shape[1:], F32),) * modes
    states = absorb(states, mix(0, [x_ref.at[0], before_ref.at[1], before_ref.at[0]]))
    states = absorb(states, mix(1, [x_ref.at[1], x_ref.at[0], before_ref.at[1]]))
    states = lax.fori_loop(2, tokens, step, states, unroll=3)
    for n in range(modes):
        state_ref[n] = states[n]


def incoming(rates, arrived, reach_ref, n):
    terms = []
    for k, block in enumerate(arrived):
        terms.append(jnp.exp(-rates * reach_ref[0, k]) * reach_ref[1, k] * block[n])
    return tree_sum(terms)


def convolve_kernel(tokens, peers, reach_ref, rates_ref, residues_ref, mixed_ref, *refs):
    arrived, (gated_ref, convolved_ref, rows_ref) = refs[:peers], refs[peers:]
    modes, tall = rates_ref.shape[0], rates_ref.shape[1]
    decays = [jnp.exp(-rates_ref[n]) for n in range(modes)]
    weights = [residues_ref[n] * jnp.sqrt(rates_ref[n]) for n in range(modes)]
    states = tuple(incoming(rates_ref[n], arrived, reach_ref, n) for n in range(modes))

    def step(t, states):
        carried = mixed_ref[t, 1] * mixed_ref[t, 2]
        states = tuple(decays[n] * states[n] + carried for n in range(modes))
        convolved = tree_sum([weights[n] * states[n] for n in range(modes)])
        convolved_ref[t] = convolved
        rows_ref[pl.ds(pl.multiple_of(t * tall, tall), tall), :] = mixed_ref[t, 0] * convolved
        return states

    lax.fori_loop(0, tokens, step, states, unroll=4)
    for start in range(0, tokens, 16):
        for s in range(tall):
            rows = rows_ref[pl.ds(start * tall + s, 16, stride=tall), :]
            gated_ref[start : start + 16, s * LANES : (s + 1) * LANES] = rows.astype(BF16)


def back_state_kernel(tokens, peers, rates_ref, mixed_ref, convolved_ref, own_ref, *refs):
    sources, (grads_ref, state_ref, head_ref) = refs[:peers], refs[peers : peers + 3]
    terms, sems = refs[peers + 3 : -1], refs[-1]
    copies = []
    for k in range(peers):
        copies.append(pltpu.make_async_copy(sources[k], terms[k], sems.at[k]))
        copies[k].start()
    modes, tall = rates_ref.shape[0], rates_ref.shape[1]
    decays = [jnp.exp(-rates_ref[n]) for n in range(modes)]
    for copy in copies:
        copy.wait()
    for start in range(0, tokens, 16):
        for s in range(tall):
            lanes = slice(s * LANES, (s + 1) * LANES)
            parts = [term[start : start + 16, lanes].astype(F32) for term in terms]
            total = tree_sum([own_ref[start : start + 16, lanes]] + parts)
            grads_ref[pl.ds(start * tall + s, 16, stride=tall), :] = total

    def step(i, states):
        t = tokens - 1 - i
        here = grads_ref[pl.ds(pl.multiple_of(t * tall, tall), tall), :] * mixed_ref[t, 0]
        return tuple(decays[n] * states[n] + here for n in range(modes))

    empty = jnp.zeros(state_ref.shape[1:], F32)
    states = lax.fori_loop(0, tokens, step, (empty,) * modes, unroll=4)
    for n in range(modes):
        state_ref[n] = states[n]
    for t in range(2):
        head_ref[t, 0] = grads_ref[t * tall : (t + 1) * tall, :]
        head_ref[t, 1] = convolved_ref[t]
        for j in range(3):
            head_ref[t, 2 + j] = mixed_ref[t, j]


def adjoint_kernel(
    tokens, peers, reach_ref, rates_ref, residues_ref, taps_ref, mixed_ref, convolved_ref,
    grads_ref, after_ref, *refs
):
    arrived, (out_ref,) = refs[:peers], refs[peers:]
    modes, tall = rates_ref.shape[0], rates_ref.shape[1]
    decays = [jnp.exp(-rates_ref[n]) for n in range(modes)]
    weights = [residues_ref[n] * jnp.sqrt(rates_ref[n]) for n in range(modes)]

    def spread(grad, convolved, mixed, states):
        grad_carried = tree_sum([weights[n] * states[n] for n in range(modes)])
        return (grad * convolved, grad_carried * mixed[2], grad_carried * mixed[1])

    def spread_after(t, states):
        mixed = [after_ref[t, 2 + j] for j in range(3)]
        return spread(after_ref[t, 0], after_ref[t, 1], mixed, states)

    states = tuple(incoming(rates_ref[n], arrived, reach_ref, n) for n in range(modes))
    first = spread_after(0, states)
    beyond = after_ref[0, 0] * after_ref[0, 2]
    second = spread_after(
        1, tuple((states[n] - beyond) * jnp.exp(rates_ref[n]) for n in range(modes))
    )

    def step(i, carry):
        states, first, second = carry
        t = tokens - 1 - i
        grad = grads_ref[pl.ds(pl.multiple_of(t * tall, tall), tall), :]
        here = grad * mixed_ref[t, 0]
        states = tuple(decays[n] * states[n] + here for n in range(modes))
        mine = spread(grad, convolved_ref[t], mixed_ref.at[t], states)
        for j in range(3):
            out_ref[t, j] = (
                taps_ref[0, j] * mine[j] + taps_ref[1, j] * first[j] + taps_ref[2, j] * second[j]
            )
        return states, mine, first

    lax.fori_loop(0, tokens, step, (states, first, second), unroll=4)


def fetched(pairs, sems):
    copies = []
    for source, target in pairs:
        copies.append(pltpu.make_async_copy(source, target, sems.at[len(copies)]))
        copies[-1].start()
    return copies


def stacked(pieces, target):
    pairs, at = [], 0
    for piece in pieces:
        pairs.append((piece, target.at[pl.ds(at, piece.shape[0]), :]))
        at += piece.shape[0]
    return pairs


def product_kernel(n_pair, n_line, pieces, place_ref, own_src, mine_src, *refs):
    others, arrived = refs[:pieces], refs[pieces : pieces + 4]
    blocks, outs = refs[pieces + 4 : pieces + 4 + n_pair], refs[pieces + 4 + n_pair : -6]
    own_ref, other_ref, rows_ref, gated_ref, half_ref, sems = refs[-6:]
    core, turn, side, pair = [place_ref[i] for i in range(4)]
    tokens, (wide, width) = mine_src.shape[0], own_src.shape
    part = tokens // 4
    columns = pl.ds(pl.multiple_of(pair * 2 * width, 2 * width), 2 * width)
    rows = [(mine_src.at[:, columns], rows_ref.at[pl.ds(0, tokens), :])]
    turns = (2 * turn, 2 * (1 - turn), 2 * turn, 2 * (1 - turn))
    cores = (core, core, 1 - core, 1 - core)
    for k in range(1, n_pair):
        for block, up, across in zip(arrived, turns, cores):
            at = pl.multiple_of(k * tokens + (up + across) * part, part)
            source = block.at[pl.ds((k - 1) * part, part), :]
            rows.append((source, rows_ref.at[pl.ds(at, part), :]))
    pairs = [(own_src, own_ref)] + stacked(blocks, gated_ref)
    first, pairs = len(pairs), pairs + rows
    second, pairs = len(pairs), pairs + stacked(others, other_ref)
    copies = fetched(pairs, sems)
    contract = (((1,), (1,)), ((), ()))
    tall = n_line * tokens

    def project(w_ref, at):
        step = min(256, width)
        for out_ref, half in ((outs[0], 1 - core), (outs[1], core)):
            rows = gated_ref[pl.ds(pl.multiple_of(half * tall, tall), tall), :]
            for n in range(0, width, step):
                product = jnp.dot(rows, w_ref[:, n : n + step], preferred_element_type=F32)
                columns = pl.ds(pl.multiple_of(at * width + n, step), step)
                out_ref[:, columns] = product.astype(BF16)

    def pull(w_ref, at, n, step):
        rows = rows_ref[:, pl.ds(pl.multiple_of(at * width, width), width)]
        w = w_ref[n : n + step, :]
        return lax.dot_general(rows, w, contract, preferred_element_type=F32)

    for copy in copies[:first]:
        copy.wait()
    project(own_ref, side)
    for copy in copies[first:second]:
        copy.wait()
    step = min(256, wide)
    for n in range(0, wide, step):
        half_ref[:, n : n + step] = pull(own_ref, side, n, step)
    for copy in copies[second:]:
        copy.wait()
    for n in range(0, wide, step):
        total = half_ref[:, n : n + step] + pull(other_ref, 1 - side, n, step)
        for k, out_ref in enumerate(outs[2:]):
            here = total[k * tokens : (k + 1) * tokens]
            out_ref[:, n : n + step] = here.astype(out_ref.dtype)
    project(other_ref, 1 - side)


def per_device(featurized, short_taps, residues, decay_rates, w_out, grad_out):
    tokens, _, wide = featurized.shape
    tall = wide // LANES
    modes = residues.shape[1]
    n_ctx, n_fsdp = lax.axis_size("ctx"), lax.axis_size("fsdp")
    me, group = lax.axis_index("ctx"), lax.axis_index("fsdp")
    pair, side = me // 2, me % 2
    core, line = group % 2, group // 2
    n_pair, n_line = n_ctx // 2, n_fsdp // 2
    width = w_out.shape[1]
    turn, part = line % 2, tokens // 4
    place = jnp.stack([core, turn, side, pair]).astype(jnp.int32)

    before = shifted(featurized[tokens - 2 :], "ctx", 1)

    near_cut = []
    for k in range(1, n_pair):
        at = ((2 * turn + core) * part, (pair ^ k) * 2 * width)
        block = lax.dynamic_slice(grad_out, at, (part, 2 * width))
        near_cut.append(block)

    def tiled(rows):
        return rows.astype(F32).reshape(-1, 3, tall, LANES)

    taps = tiled(short_taps)
    rates = decay_rates.T.reshape(modes, tall, LANES)
    weights = residues.T.reshape(modes, tall, LANES)
    state_shape = jax.ShapeDtypeStruct((modes, tall, LANES), F32)
    levels = range(n_ctx.bit_length() - 1)
    uppers = [(me >> b) % 2 for b in levels]
    belows = [me % (1 << b) for b in levels]

    def exchanged(total, later, others=()):
        arrived = []
        for b in levels:
            partner = swapped(total, "ctx", 1 << b)
            if others and b == 0:
                partner, others = lax.optimization_barrier((partner, others))
            arrived.append(partner)
            if b + 1 < len(levels):
                decay = jnp.exp(-rates * (tokens << b))
                fades = (uppers[b] == 0) == later
                total = jnp.where(fades, total * decay + partner, partner * decay + total)
        return (arrived, others) if others else arrived

    reach = jnp.stack([
        jnp.stack([below * tokens for below in belows]),
        jnp.stack([upper == 1 for upper in uppers]),
    ]).astype(F32)
    back_reach = jnp.stack([
        jnp.stack([((1 << b) - 1 - belows[b]) * tokens for b in levels]),
        jnp.stack([upper == 0 for upper in uppers]),
    ]).astype(F32)

    mixed, state = kernel_call(
        functools.partial(chunk_state_kernel, tokens),
        (jax.ShapeDtypeStruct((tokens, 3, tall, LANES), F32), state_shape),
        [VMEM] * 4,
        flops=50 * tokens * wide,
        moved=8 * tokens * 3 * wide,
    )(tiled(featurized), tiled(before), taps, rates)
    w_held, state = lax.optimization_barrier((w_out, state))
    arrived = exchanged(state, True)
    w_held, _ = lax.optimization_barrier((w_out, arrived[0]))
    w_other = [swapped(w_held, "ctx", 1)]
    near_cut, _ = lax.optimization_barrier((near_cut, arrived[2]))
    near = [swapped(block, "ctx", 2 * k) for k, block in enumerate(near_cut, 1)]
    gated, convolved = kernel_call(
        functools.partial(convolve_kernel, tokens, len(arrived)),
        (
            jax.ShapeDtypeStruct((tokens, wide), BF16),
            jax.ShapeDtypeStruct((tokens, tall, LANES), F32),
        ),
        [SMEM] + [VMEM] * (3 + len(arrived)),
        [pltpu.VMEM((tokens * tall, LANES), F32)],
        flops=64 * tokens * wide,
        moved=8 * tokens * 3 * wide,
    )(reach, rates, weights, mixed, *arrived)

    blocks = [gated] + [swapped(gated, "ctx", 2 * k) for k in range(1, n_pair)]
    near, _ = lax.optimization_barrier((near, gated))
    near = jnp.concatenate(near, axis=0)
    across = swapped(near, "fsdp", 2)
    far = [swapped(near, "fsdp", 1), swapped(across, "fsdp", 1)]

    route = []
    for f in range(n_fsdp):
        for p in range(n_pair):
            for x in range(2):
                target = p ^ ((f % 2) * n_line + f // 2)
                route.append((f * n_ctx + 2 * p + x, p * n_ctx + 2 * target + x))

    halved = jax.ShapeDtypeStruct((n_line * tokens, 2 * width), BF16)
    given, kept, *outs = kernel_call(
        functools.partial(product_kernel, n_pair, n_line, len(w_other)),
        (halved, halved, jax.ShapeDtypeStruct((tokens, wide), F32))
        + (jax.ShapeDtypeStruct((tokens, wide), BF16),) * (n_pair - 1),
        [SMEM] + [HBM] * (2 + len(w_other)) + [ANYWHERE] * (4 + n_pair),
        [
            pltpu.VMEM((wide, width), BF16),
            pltpu.VMEM((wide, width), BF16),
            pltpu.VMEM((n_pair * tokens, 2 * width), BF16),
            pltpu.VMEM((n_pair * tokens, wide), BF16),
            pltpu.VMEM((n_pair * tokens, wide), F32),
            pltpu.SemaphoreType.DMA((2 + 4 * (n_pair - 1) + len(w_other) + n_pair,)),
        ],
        flops=8 * n_pair * tokens * wide * width,
        moved=8 * wide * width,
    )(place, w_out, grad_out, *w_other, near, across, *far, *blocks)
    terms = [outs[0]] + [swapped(outs[k], "ctx", 2 * k) for k in range(1, n_pair)]

    sent = swapped(given, "fsdp", 1).reshape(n_line, tokens, 2 * width)
    kept = kept.reshape(n_line, tokens, 2 * width)

    def summed(at):
        pieces = [lax.dynamic_index_in_dim(x, at, 0, False).astype(F32) for x in (kept, sent)]
        return pieces[0] + pieces[1]

    total = summed(line)
    rest = [summed(line ^ m).astype(BF16) for m in range(1, n_line)]
    gathered = []
    for at in (0, width):
        part = total[:, at : at + width]
        for m, block in enumerate(rest, 1):
            part = part + swapped(block[:, at : at + width], "fsdp", 2 * m).astype(F32)
        gathered.append(part.astype(BF16))
    terms, _ = lax.optimization_barrier((terms, gathered))
    placed = [lax.ppermute(part, ("fsdp", "ctx"), route) for part in gathered]

    grads, back_state, head = kernel_call(
        functools.partial(back_state_kernel, tokens, n_pair - 1),
        (
            jax.ShapeDtypeStruct((tokens * tall, LANES), F32),
            state_shape,
            jax.ShapeDtypeStruct((2, 5, tall, LANES), F32),
        ),
        [VMEM] * 4 + [ANYWHERE] * (n_pair - 1),
        [pltpu.VMEM((tokens, wide), BF16)] * (n_pair - 1)
        + [pltpu.SemaphoreType.DMA((n_pair - 1,))],
        flops=40 * tokens * wide,
        moved=8 * tokens * 3 * wide,
    )(rates, mixed, convolved, *terms)
    back_arrived, placed = exchanged(back_state, False, placed)
    block_output = jnp.concatenate(placed, axis=1)
    following = shifted(head, "ctx", -1)
    out = kernel_call(
        functools.partial(adjoint_kernel, tokens, len(back_arrived)),
        (jax.ShapeDtypeStruct((tokens, 3, tall, LANES), F32),),
        [SMEM] + [VMEM] * (7 + len(back_arrived)),
        flops=80 * tokens * wide,
        moved=8 * tokens * 3 * wide,
    )(back_reach, rates, weights, taps, mixed, convolved, grads, following, *back_arrived)[0]
    grad_features = out.reshape(tokens, 3, wide).astype(BF16)
    return (block_output, grad_features)


def solution(mesh):
    placed = (
        P("ctx", None, "fsdp"),
        P(None, None, "fsdp"),
        P("fsdp", None),
        P("fsdp", None),
        P("fsdp", "ctx"),
        P("ctx", None),
    )
    return jax.shard_map(
        per_device,
        mesh=mesh,
        in_specs=placed,
        out_specs=(P("ctx", "fsdp"), P("ctx", None, "fsdp")),
        check_vma=False,
    )
```

```python
import functools

import jax
import jax.numpy as jnp
from jax import lax
from jax.experimental import pallas as pl
from jax.experimental.pallas import tpu as pltpu
from jax.sharding import PartitionSpec as P

LANES = 128
F32 = jnp.float32
BF16 = jnp.bfloat16
VMEM = pl.BlockSpec(memory_space=pltpu.VMEM)
SMEM = pl.BlockSpec(memory_space=pltpu.SMEM)
HBM = pl.BlockSpec(memory_space=pltpu.HBM)
ANYWHERE = pl.BlockSpec(memory_space=pl.ANY)


def swapped(block, axis, mask):
    count = lax.axis_size(axis)
    return lax.ppermute(block, axis, [(i, i ^ mask) for i in range(count)])


def shifted(block, axis, distance):
    devices = range(lax.axis_size(axis))
    route = [(i - distance, i) for i in devices if i - distance in devices]
    return lax.ppermute(block, axis, route)


def tree_sum(terms):
    terms = list(terms)
    while len(terms) > 1:
        paired = [terms[i] + terms[i + 1] for i in range(0, len(terms) - 1, 2)]
        terms = paired + terms[len(terms) - len(terms) % 2 :]
    return terms[0]


def kernel_call(body, out_shape, in_specs, scratch_shapes=(), flops=0, moved=0):
    return pl.pallas_call(
        body,
        out_shape=out_shape,
        in_specs=in_specs,
        out_specs=jax.tree.map(lambda _: VMEM, out_shape),
        scratch_shapes=scratch_shapes,
        compiler_params=pltpu.CompilerParams(vmem_limit_bytes=48 * 1024 * 1024),
        cost_estimate=pl.CostEstimate(flops=flops, bytes_accessed=moved, transcendentals=0),
    )


def chunk_state_kernel(tokens, x_ref, before_ref, taps_ref, rates_ref, mixed_ref, state_ref):
    modes = rates_ref.shape[0]
    decays = [jnp.exp(-rates_ref[n]) for n in range(modes)]

    def mix(t, rows):
        parts = []
        for j in range(3):
            part = tree_sum([taps_ref[i, j] * rows[i][j] for i in range(3)])
            mixed_ref[t, j] = part
            parts.append(part)
        return parts[1] * parts[2]

    def absorb(states, carried):
        return tuple(decays[n] * states[n] + carried for n in range(modes))

    def step(t, states):
        return absorb(states, mix(t, [x_ref.at[t - i] for i in range(3)]))

    states = (jnp.zeros(state_ref.shape[1:], F32),) * modes
    states = absorb(states, mix(0, [x_ref.at[0], before_ref.at[1], before_ref.at[0]]))
    states = absorb(states, mix(1, [x_ref.at[1], x_ref.at[0], before_ref.at[1]]))
    states = lax.fori_loop(2, tokens, step, states, unroll=3)
    for n in range(modes):
        state_ref[n] = states[n]


def incoming(rates, arrived, reach_ref, n):
    terms = []
    for k, block in enumerate(arrived):
        terms.append(jnp.exp(-rates * reach_ref[0, k]) * reach_ref[1, k] * block[n])
    return tree_sum(terms)


def convolve_kernel(tokens, peers, reach_ref, rates_ref, residues_ref, mixed_ref, *refs):
    arrived, (gated_ref, convolved_ref, rows_ref) = refs[:peers], refs[peers:]
    modes, tall = rates_ref.shape[0], rates_ref.shape[1]
    decays = [jnp.exp(-rates_ref[n]) for n in range(modes)]
    weights = [residues_ref[n] * jnp.sqrt(rates_ref[n]) for n in range(modes)]
    states = tuple(incoming(rates_ref[n], arrived, reach_ref, n) for n in range(modes))

    def step(t, states):
        carried = mixed_ref[t, 1] * mixed_ref[t, 2]
        states = tuple(decays[n] * states[n] + carried for n in range(modes))
        convolved = tree_sum([weights[n] * states[n] for n in range(modes)])
        convolved_ref[t] = convolved
        rows_ref[pl.ds(pl.multiple_of(t * tall, tall), tall), :] = mixed_ref[t, 0] * convolved
        return states

    lax.fori_loop(0, tokens, step, states, unroll=4)
    for start in range(0, tokens, 16):
        for s in range(tall):
            rows = rows_ref[pl.ds(start * tall + s, 16, stride=tall), :]
            gated_ref[start : start + 16, s * LANES : (s + 1) * LANES] = rows.astype(BF16)


def back_state_kernel(tokens, peers, rates_ref, mixed_ref, convolved_ref, own_ref, *refs):
    sources, (grads_ref, state_ref, head_ref) = refs[:peers], refs[peers : peers + 3]
    terms, sems = refs[peers + 3 : -1], refs[-1]
    copies = []
    for k in range(peers):
        copies.append(pltpu.make_async_copy(sources[k], terms[k], sems.at[k]))
        copies[k].start()
    modes, tall = rates_ref.shape[0], rates_ref.shape[1]
    decays = [jnp.exp(-rates_ref[n]) for n in range(modes)]
    for copy in copies:
        copy.wait()
    for start in range(0, tokens, 16):
        for s in range(tall):
            lanes = slice(s * LANES, (s + 1) * LANES)
            parts = [term[start : start + 16, lanes].astype(F32) for term in terms]
            total = tree_sum([own_ref[start : start + 16, lanes]] + parts)
            grads_ref[pl.ds(start * tall + s, 16, stride=tall), :] = total

    def step(i, states):
        t = tokens - 1 - i
        here = grads_ref[pl.ds(pl.multiple_of(t * tall, tall), tall), :] * mixed_ref[t, 0]
        return tuple(decays[n] * states[n] + here for n in range(modes))

    empty = jnp.zeros(state_ref.shape[1:], F32)
    states = lax.fori_loop(0, tokens, step, (empty,) * modes, unroll=4)
    for n in range(modes):
        state_ref[n] = states[n]
    for t in range(2):
        head_ref[t, 0] = grads_ref[t * tall : (t + 1) * tall, :]
        head_ref[t, 1] = convolved_ref[t]
        for j in range(3):
            head_ref[t, 2 + j] = mixed_ref[t, j]


def adjoint_kernel(
    tokens, peers, reach_ref, rates_ref, residues_ref, taps_ref, mixed_ref, convolved_ref,
    grads_ref, after_ref, *refs
):
    arrived, (out_ref,) = refs[:peers], refs[peers:]
    modes, tall = rates_ref.shape[0], rates_ref.shape[1]
    decays = [jnp.exp(-rates_ref[n]) for n in range(modes)]
    weights = [residues_ref[n] * jnp.sqrt(rates_ref[n]) for n in range(modes)]

    def spread(grad, convolved, mixed, states):
        grad_carried = tree_sum([weights[n] * states[n] for n in range(modes)])
        return (grad * convolved, grad_carried * mixed[2], grad_carried * mixed[1])

    def spread_after(t, states):
        mixed = [after_ref[t, 2 + j] for j in range(3)]
        return spread(after_ref[t, 0], after_ref[t, 1], mixed, states)

    states = tuple(incoming(rates_ref[n], arrived, reach_ref, n) for n in range(modes))
    first = spread_after(0, states)
    beyond = after_ref[0, 0] * after_ref[0, 2]
    second = spread_after(
        1, tuple((states[n] - beyond) * jnp.exp(rates_ref[n]) for n in range(modes))
    )

    def step(i, carry):
        states, first, second = carry
        t = tokens - 1 - i
        grad = grads_ref[pl.ds(pl.multiple_of(t * tall, tall), tall), :]
        here = grad * mixed_ref[t, 0]
        states = tuple(decays[n] * states[n] + here for n in range(modes))
        mine = spread(grad, convolved_ref[t], mixed_ref.at[t], states)
        for j in range(3):
            out_ref[t, j] = (
                taps_ref[0, j] * mine[j] + taps_ref[1, j] * first[j] + taps_ref[2, j] * second[j]
            )
        return states, mine, first

    lax.fori_loop(0, tokens, step, (states, first, second), unroll=4)


def fetched(pairs, sems):
    copies = []
    for source, target in pairs:
        copies.append(pltpu.make_async_copy(source, target, sems.at[len(copies)]))
        copies[-1].start()
    return copies


def stacked(pieces, target):
    pairs, at = [], 0
    for piece in pieces:
        pairs.append((piece, target.at[pl.ds(at, piece.shape[0]), :]))
        at += piece.shape[0]
    return pairs


def product_kernel(n_pair, n_line, pieces, place_ref, own_src, mine_src, *refs):
    others, arrived = refs[:pieces], refs[pieces : pieces + 4]
    blocks, outs = refs[pieces + 4 : pieces + 4 + n_pair], refs[pieces + 4 + n_pair : -6]
    own_ref, other_ref, rows_ref, gated_ref, half_ref, sems = refs[-6:]
    core, turn, side, pair = [place_ref[i] for i in range(4)]
    tokens, (wide, width) = mine_src.shape[0], own_src.shape
    part = tokens // 4
    columns = pl.ds(pl.multiple_of(pair * 2 * width, 2 * width), 2 * width)
    rows = [(mine_src.at[:, columns], rows_ref.at[pl.ds(0, tokens), :])]
    turns = (2 * turn, 2 * (1 - turn), 2 * turn, 2 * (1 - turn))
    cores = (core, core, 1 - core, 1 - core)
    for k in range(1, n_pair):
        for block, up, across in zip(arrived, turns, cores):
            at = pl.multiple_of(k * tokens + (up + across) * part, part)
            source = block.at[pl.ds((k - 1) * part, part), :]
            rows.append((source, rows_ref.at[pl.ds(at, part), :]))
    pairs = [(own_src, own_ref)] + stacked(blocks, gated_ref)
    first, pairs = len(pairs), pairs + rows
    second, pairs = len(pairs), pairs + stacked(others, other_ref)
    copies = fetched(pairs, sems)
    contract = (((1,), (1,)), ((), ()))
    tall = n_line * tokens

    def project(w_ref, at):
        step = min(256, width)
        for out_ref, half in ((outs[0], 1 - core), (outs[1], core)):
            rows = gated_ref[pl.ds(pl.multiple_of(half * tall, tall), tall), :]
            for n in range(0, width, step):
                product = jnp.dot(rows, w_ref[:, n : n + step], preferred_element_type=F32)
                columns = pl.ds(pl.multiple_of(at * width + n, step), step)
                out_ref[:, columns] = product.astype(BF16)

    def pull(w_ref, at, n, step):
        rows = rows_ref[:, pl.ds(pl.multiple_of(at * width, width), width)]
        w = w_ref[n : n + step, :]
        return lax.dot_general(rows, w, contract, preferred_element_type=F32)

    for copy in copies[:first]:
        copy.wait()
    project(own_ref, side)
    for copy in copies[first:second]:
        copy.wait()
    step = min(256, wide)
    for n in range(0, wide, step):
        half_ref[:, n : n + step] = pull(own_ref, side, n, step)
    for copy in copies[second:]:
        copy.wait()
    for n in range(0, wide, step):
        total = half_ref[:, n : n + step] + pull(other_ref, 1 - side, n, step)
        for k, out_ref in enumerate(outs[2:]):
            here = total[k * tokens : (k + 1) * tokens]
            out_ref[:, n : n + step] = here.astype(out_ref.dtype)
    project(other_ref, 1 - side)


def per_device(featurized, short_taps, residues, decay_rates, w_out, grad_out):
    tokens, _, wide = featurized.shape
    tall = wide // LANES
    modes = residues.shape[1]
    n_ctx, n_fsdp = lax.axis_size("ctx"), lax.axis_size("fsdp")
    me, group = lax.axis_index("ctx"), lax.axis_index("fsdp")
    pair, side = me // 2, me % 2
    core, line = group % 2, group // 2
    n_pair, n_line = n_ctx // 2, n_fsdp // 2
    width = w_out.shape[1]
    turn, part = line % 2, tokens // 4
    place = jnp.stack([core, turn, side, pair]).astype(jnp.int32)

    before = shifted(featurized[tokens - 2 :], "ctx", 1)

    near_cut = []
    for k in range(1, n_pair):
        at = ((2 * turn + core) * part, (pair ^ k) * 2 * width)
        block = lax.dynamic_slice(grad_out, at, (part, 2 * width))
        near_cut.append(block)

    def tiled(rows):
        return rows.astype(F32).reshape(-1, 3, tall, LANES)

    taps = tiled(short_taps)
    rates = decay_rates.T.reshape(modes, tall, LANES)
    weights = residues.T.reshape(modes, tall, LANES)
    state_shape = jax.ShapeDtypeStruct((modes, tall, LANES), F32)
    levels = range(n_ctx.bit_length() - 1)
    uppers = [(me >> b) % 2 for b in levels]
    belows = [me % (1 << b) for b in levels]

    def exchanged(total, later, others=()):
        arrived = []
        for b in levels:
            partner = swapped(total, "ctx", 1 << b)
            if others and b == 1:
                partner, others = lax.optimization_barrier((partner, others))
            arrived.append(partner)
            if b + 1 < len(levels):
                decay = jnp.exp(-rates * (tokens << b))
                fades = (uppers[b] == 0) == later
                total = jnp.where(fades, total * decay + partner, partner * decay + total)
        return (arrived, others) if others else arrived

    reach = jnp.stack([
        jnp.stack([below * tokens for below in belows]),
        jnp.stack([upper == 1 for upper in uppers]),
    ]).astype(F32)
    back_reach = jnp.stack([
        jnp.stack([((1 << b) - 1 - belows[b]) * tokens for b in levels]),
        jnp.stack([upper == 0 for upper in uppers]),
    ]).astype(F32)

    mixed, state = kernel_call(
        functools.partial(chunk_state_kernel, tokens),
        (jax.ShapeDtypeStruct((tokens, 3, tall, LANES), F32), state_shape),
        [VMEM] * 4,
        flops=50 * tokens * wide,
        moved=8 * tokens * 3 * wide,
    )(tiled(featurized), tiled(before), taps, rates)
    w_held, state = lax.optimization_barrier((w_out, state))
    arrived = exchanged(state, True)
    w_held, _ = lax.optimization_barrier((w_out, arrived[0]))
    w_other = [swapped(w_held, "ctx", 1)]
    near_cut, _ = lax.optimization_barrier((near_cut, arrived[2]))
    near = [swapped(block, "ctx", 2 * k) for k, block in enumerate(near_cut, 1)]
    gated, convolved = kernel_call(
        functools.partial(convolve_kernel, tokens, len(arrived)),
        (
            jax.ShapeDtypeStruct((tokens, wide), BF16),
            jax.ShapeDtypeStruct((tokens, tall, LANES), F32),
        ),
        [SMEM] + [VMEM] * (3 + len(arrived)),
        [pltpu.VMEM((tokens * tall, LANES), F32)],
        flops=64 * tokens * wide,
        moved=8 * tokens * 3 * wide,
    )(reach, rates, weights, mixed, *arrived)

    blocks = [gated] + [swapped(gated, "ctx", 2 * k) for k in range(1, n_pair)]
    near, _ = lax.optimization_barrier((near, gated))
    near = jnp.concatenate(near, axis=0)
    across = swapped(near, "fsdp", 2)
    far = [swapped(near, "fsdp", 1), swapped(across, "fsdp", 1)]

    route = []
    for f in range(n_fsdp):
        for p in range(n_pair):
            for x in range(2):
                target = p ^ ((f % 2) * n_line + f // 2)
                route.append((f * n_ctx + 2 * p + x, p * n_ctx + 2 * target + x))

    halved = jax.ShapeDtypeStruct((n_line * tokens, 2 * width), BF16)
    given, kept, *outs = kernel_call(
        functools.partial(product_kernel, n_pair, n_line, len(w_other)),
        (halved, halved, jax.ShapeDtypeStruct((tokens, wide), F32))
        + (jax.ShapeDtypeStruct((tokens, wide), BF16),) * (n_pair - 1),
        [SMEM] + [HBM] * (2 + len(w_other)) + [ANYWHERE] * (4 + n_pair),
        [
            pltpu.VMEM((wide, width), BF16),
            pltpu.VMEM((wide, width), BF16),
            pltpu.VMEM((n_pair * tokens, 2 * width), BF16),
            pltpu.VMEM((n_pair * tokens, wide), BF16),
            pltpu.VMEM((n_pair * tokens, wide), F32),
            pltpu.SemaphoreType.DMA((2 + 4 * (n_pair - 1) + len(w_other) + n_pair,)),
        ],
        flops=8 * n_pair * tokens * wide * width,
        moved=8 * wide * width,
    )(place, w_out, grad_out, *w_other, near, across, *far, *blocks)
    terms = [outs[0]] + [swapped(outs[k], "ctx", 2 * k) for k in range(1, n_pair)]

    sent = swapped(given, "fsdp", 1).reshape(n_line, tokens, 2 * width)
    kept = kept.reshape(n_line, tokens, 2 * width)

    def summed(at):
        pieces = [lax.dynamic_index_in_dim(x, at, 0, False).astype(F32) for x in (kept, sent)]
        return pieces[0] + pieces[1]

    total = summed(line)
    rest = [summed(line ^ m).astype(BF16) for m in range(1, n_line)]
    gathered = []
    for at in (0, width):
        part = total[:, at : at + width]
        for m, block in enumerate(rest, 1):
            part = part + swapped(block[:, at : at + width], "fsdp", 2 * m).astype(F32)
        gathered.append(part.astype(BF16))
    placed = [lax.ppermute(part, ("fsdp", "ctx"), route) for part in gathered]

    grads, back_state, head = kernel_call(
        functools.partial(back_state_kernel, tokens, n_pair - 1),
        (
            jax.ShapeDtypeStruct((tokens * tall, LANES), F32),
            state_shape,
            jax.ShapeDtypeStruct((2, 5, tall, LANES), F32),
        ),
        [VMEM] * 4 + [ANYWHERE] * (n_pair - 1),
        [pltpu.VMEM((tokens, wide), BF16)] * (n_pair - 1)
        + [pltpu.SemaphoreType.DMA((n_pair - 1,))],
        flops=40 * tokens * wide,
        moved=8 * tokens * 3 * wide,
    )(rates, mixed, convolved, *terms)
    back_arrived, placed = exchanged(back_state, False, placed)
    block_output = jnp.concatenate(placed, axis=1)
    following = shifted(head, "ctx", -1)
    out = kernel_call(
        functools.partial(adjoint_kernel, tokens, len(back_arrived)),
        (jax.ShapeDtypeStruct((tokens, 3, tall, LANES), F32),),
        [SMEM] + [VMEM] * (7 + len(back_arrived)),
        flops=80 * tokens * wide,
        moved=8 * tokens * 3 * wide,
    )(back_reach, rates, weights, taps, mixed, convolved, grads, following, *back_arrived)[0]
    grad_features = out.reshape(tokens, 3, wide).astype(BF16)
    return (block_output, grad_features)


def solution(mesh):
    placed = (
        P("ctx", None, "fsdp"),
        P(None, None, "fsdp"),
        P("fsdp", None),
        P("fsdp", None),
        P("fsdp", "ctx"),
        P("ctx", None),
    )
    return jax.shard_map(
        per_device,
        mesh=mesh,
        in_specs=placed,
        out_specs=(P("ctx", "fsdp"), P("ctx", None, "fsdp")),
        check_vma=False,
    )
```
